32 devices in a mesh: rep: 2 (over x), node: 2 (over core), local: 8 (over z, y).
Axes of the slice: x: 2, y: 2, z: 4, core: 2. Of those that a mesh axis runs over, the one named last changes fastest.
Arguments:
- hidden_rows: bfloat16 [256, 7168], P(('rep', 'node', 'local')), parts along dimension 0, may hold values from -6 to 6
- w_router: bfloat16 [7168, 8], replicated, may hold values from -0.0625 to 0.0625
- chosen: int32 [256, 4], P(('rep', 'node', 'local')), parts along dimension 0, may hold values from 0 to 7, all different within a row; in each aligned block of 8 rows (0 to 7, 8 to 15, ...) at most 6 rows name the same one
- w_gate: bfloat16 [7168, 16384], P(None, ('node', 'local')), may hold values from -0.0625 to 0.0625
- w_up: bfloat16 [7168, 16384], P(None, ('node', 'local')), may hold values from -0.0625 to 0.0625
- w_down: bfloat16 [16384, 7168], P(('node', 'local')), may hold values from -0.125 to 0.125
- q_latent: bfloat16 [64, 65536], P(('rep', 'node', 'local')), parts along dimension 0, may hold values from -73 to 73
- q_rope: bfloat16 [64, 8192], P(('rep', 'node', 'local')), parts along dimension 0, may hold values from -4 to 4
- cache_latent: bfloat16 [64, 512, 512], P(('rep', 'node', 'local')), parts along dimension 0, may hold values from -4 to 4
- cache_rope: bfloat16 [64, 64, 512], P(('rep', 'node', 'local')), parts along dimension 0, may hold values from -4 to 4
- lengths: int32 [64], P(('rep', 'node', 'local')), parts along dimension 0, may hold values from 64 to 512, as said below
Outputs:
- moe_out: bfloat16 [256, 7168], P(('rep', 'node', 'local')), parts along dimension 0
- context: bfloat16 [64, 65536], P(('rep', 'node', 'local')), parts along dimension 0
The draws below stay inside these ranges and needn't reach their ends.
There are 2 independent parts, one for each index of `rep`. The reference program is written for one: setup_inputs(seed, part) draws one part's arguments, and reference() takes and returns one part's arrays. A program takes and returns all parts, laid end to end along the dimension named above; an argument that names none is the same for every part. Nothing has to cross between parts.
Inputs may be any that keep to these rules, and one draw needn't show every extreme that they name: `chosen`: each row names 4 different experts; among the rows of one device no expert is named by more than 6 rows, a bound that some block reaches. `lengths`: some row has all 512 positions filled.
All inputs are finite; a program needn't handle non-finite values.
Results may differ from the reference program's by a relative error of at most 0.005.
Values may be sent and summed in bfloat16 or wider, within the bound.
A program may use at most 128 MiB of HBM per device.

```python
import math
import jax
import jax.numpy as jnp
import numpy as np
from jax import lax

D = 7168
TOPG = 4
EXPERT_FF = 2048
NH = 128
LAT = 512
ROPE = 64
R_DEV = 8
LMAX = 512
EXPERTS = 8
CAP = 6
ROWS = 128
BATT = 32


def shared_cache(key):
    base = jnp.clip(jax.random.normal(key, (BATT, LMAX, LAT), jnp.float32), -4.0, 4.0)
    return base.at[:, 3, :].set(base[:, 3, :])


def draw_cache_latent(key, part):
    shared = shared_cache(key)
    return shared.astype(jnp.bfloat16)


def draw_q_latent(key, part):
    key = jax.random.fold_in(key, 5)
    base = jnp.clip(jax.random.normal(key, (BATT, NH, LAT), jnp.float32), -4.0, 4.0)
    return base.reshape(BATT, NH * LAT).astype(jnp.bfloat16)


def draw_lengths(key, part):
    key = jax.random.fold_in(key, 7)
    spread = jax.random.randint(key, (BATT,), LMAX // 8, LMAX + 1)
    return spread.at[0].set(LMAX).astype(jnp.int32)


def levels(rng, shape, shards, smallest, largest):
    level = 1.0
    for position, shards_of in shards:
        draws = jax.random.uniform(jax.random.fold_in(jax.random.fold_in(rng, 6), position), (shards_of,), jnp.float32, smallest / len(shards), largest / len(shards))
        level = level * jnp.repeat(jnp.exp(draws), shape[position] // shards_of).reshape((-1,) + (1,) * (len(shape) - 1 - position))
    return level


def routed_block(key, own, number, rows, amount, top, reach, lean):
    ranking = jax.random.permutation(key, amount)
    crowded, usual = shares(amount, rows * top, reach, lean, True), shares(amount, rows * top, reach, lean, False)
    places = jnp.arange(amount)

    def named(tallies, turn):
        used = int((tallies > 0).sum())
        fixed = max(1, used // 4)
        moved = fixed + (places - fixed + turn * (used - fixed)) % max(1, amount - fixed)
        return jnp.zeros((amount,), jnp.int32).at[ranking[jnp.where(places < fixed, places, moved)]].set(jnp.asarray(tallies, jnp.int32))

    tallies = jnp.where(number % 4 == 0, named(crowded, number // 4), named(usual, number - number // 4 - 1))
    mixed = jax.random.permutation(jax.random.fold_in(own, 3), amount)
    source_of, taker = mixed[0:amount // 2 * 2:2], mixed[1:amount // 2 * 2:2]
    margin = jnp.minimum(tallies[source_of] - 1, reach - tallies[taker]) // 2
    margin = jnp.where((source_of == ranking[0]) | (taker == ranking[0]) | (tallies[taker] == 0), 0, jnp.maximum(margin, 0))
    moved = jax.random.randint(jax.random.fold_in(own, 4), (amount // 2,), 0, 1 << 20) % (margin + 1)
    tallies = tallies.at[source_of].add(-moved).at[taker].add(moved)
    labels = jnp.searchsorted(jnp.cumsum(tallies), jnp.arange(rows * top), side="right").astype(jnp.int32)
    table = labels.reshape(top, rows).T
    table = table[jax.random.permutation(jax.random.fold_in(own, 1), rows)]
    turn = jax.random.randint(jax.random.fold_in(own, 2), (rows, 1), 0, top)
    return jnp.take_along_axis(table, (jnp.arange(top)[None, :] + turn) % top, axis=1)


def shares(amount, total, most, skew, full):
    weights = [(1 << 20) // math.isqrt(standing ** skew) + 1 for standing in range(1, amount + 1)]
    largest = most if full else min(most, max(-(-total // amount), total * weights[0] // sum(weights)))
    least = 1 if total - largest >= amount - 1 else 0
    given, rest = [largest] + [least] * (amount - 1), total - largest - least * (amount - 1)
    while rest > 0:
        candidates = [i for i in range(1, amount) if given[i] < largest] or [i for i in range(1, amount) if given[i] < most]
        mass, remaining = sum([weights[i] for i in candidates]), rest
        for i in candidates:
            extra = min(most - given[i], max(1, remaining * weights[i] // mass), rest)
            given[i] = given[i] + extra
            rest = rest - extra
    return np.array(given)


def centred(own_key, shape, scale, reach, split=(), dtype=jnp.bfloat16):
    drawn = jax.random.normal(own_key, shape, jnp.float32) * scale
    if len(split) > 0:
        drawn = levels(own_key, shape, split, -0.22, 0.18) * drawn
    return jnp.clip(drawn, min=-reach, max=reach).astype(dtype)


def setup_inputs(seed: int = 0, part: int = 0) -> dict:
    key_of = jax.random.split(jax.random.key(seed), 12)
    own_keys = jax.random.split(jax.random.fold_in(key_of[11], part), 12)
    hidden_rows = centred(own_keys[0], (ROWS, D), 1.0, 6.0, ((0, 16),))
    w_router = centred(key_of[1], (D, EXPERTS), D ** -0.5, 0.0625)
    chosen_keys = jax.random.split(jax.random.fold_in(own_keys[2], 1), ROWS // R_DEV)
    chosen_turns = jax.random.permutation(jax.random.fold_in(own_keys[2], 3), ROWS // R_DEV)
    chosen = jax.vmap(lambda own, number: routed_block(jax.random.fold_in(own_keys[2], 2), own, number, R_DEV, EXPERTS, TOPG, CAP, 2))(chosen_keys, chosen_turns).reshape((ROWS, TOPG))
    w_gate = centred(key_of[3], (D, EXPERTS * EXPERT_FF), D ** -0.5, 0.0625, ((1, 16),))
    w_up = centred(key_of[4], (D, EXPERTS * EXPERT_FF), D ** -0.5, 0.0625, ((1, 16),))
    w_down = centred(key_of[5], (EXPERTS * EXPERT_FF, D), EXPERT_FF ** -0.5, 0.125, ((0, 16),))
    q_latent = draw_q_latent(jax.random.fold_in(jax.random.fold_in(key_of[11], part), 71), part)
    q_rope = centred(own_keys[7], (BATT, NH * ROPE), 1.0, 4.0, ((0, 16),))
    cache_latent = draw_cache_latent(jax.random.fold_in(jax.random.fold_in(key_of[11], part), 71), part)
    cache_rope = centred(own_keys[9], (BATT, ROPE, LMAX), 1.0, 4.0, ((0, 16),))
    lengths = draw_lengths(jax.random.fold_in(jax.random.fold_in(key_of[11], part), 71), part)
    return dict(hidden_rows=hidden_rows, w_router=w_router, chosen=chosen, w_gate=w_gate, w_up=w_up, w_down=w_down, q_latent=q_latent, q_rope=q_rope, cache_latent=cache_latent, cache_rope=cache_rope, lengths=lengths)


route_scale = 2.5
score_scale = 192.0 ** -0.5


def attend_one(packed):
    q_lat, q_rot, cache_lat, cache_rot, filled = packed
    queries = q_lat.reshape(NH, LAT)
    rope_queries = q_rot.reshape(NH, ROPE)
    logits = jnp.dot(queries, cache_lat.T, preferred_element_type=jnp.float32)
    logits = logits + jnp.dot(rope_queries, cache_rot, preferred_element_type=jnp.float32)
    logits = logits * score_scale
    usable = (jnp.arange(LMAX) < filled)[None, :]
    logits = jnp.where(usable, logits, -1e30)
    row_peak = jnp.max(logits, axis=1, keepdims=True)
    raw_weights = jnp.exp(logits - row_peak)
    attn_probs = (raw_weights / jnp.sum(raw_weights, axis=1, keepdims=True)).astype(jnp.bfloat16)
    summed = jnp.dot(attn_probs, cache_lat, preferred_element_type=jnp.float32)
    return summed.reshape(NH * LAT).astype(jnp.bfloat16)


def reference(hidden_rows, w_router, chosen, w_gate, w_up, w_down, q_latent, q_rope, cache_latent, cache_rope, lengths):
    scores = jax.nn.sigmoid(jnp.dot(hidden_rows, w_router, preferred_element_type=jnp.float32))
    picked = jnp.take_along_axis(scores, chosen, axis=1)
    weights = route_scale * picked / jnp.sum(picked, axis=1, keepdims=True)
    mixed_sum = jnp.zeros((ROWS, D), jnp.float32)
    for expert_index in range(EXPERTS):
        first = expert_index * EXPERT_FF
        gate_act = jnp.dot(hidden_rows, w_gate[:, first:first + EXPERT_FF], preferred_element_type=jnp.float32)
        up_act = jnp.dot(hidden_rows, w_up[:, first:first + EXPERT_FF], preferred_element_type=jnp.float32)
        inner_act = (jax.nn.silu(gate_act) * up_act).astype(jnp.bfloat16)
        result = jnp.dot(inner_act, w_down[first:first + EXPERT_FF, :], preferred_element_type=jnp.float32)
        row_share = jnp.sum(jnp.where(chosen == expert_index, weights, 0.0), axis=1)
        mixed_sum = mixed_sum + row_share[:, None] * result
    moe_out = mixed_sum.astype(jnp.bfloat16)
    context = lax.map(attend_one, (q_latent, q_rope, cache_latent, cache_rope, lengths))
    return (moe_out, context)
```

```python
import functools

import jax
import jax.numpy as jnp
from jax import lax
from jax.experimental import pallas as pl
from jax.experimental.pallas import tpu as pltpu
from jax.sharding import PartitionSpec as P

EXPERTS = 8
NC = 7
PAIR = 2

route_scale = 2.5
score_scale = 192.0 ** (-0.5)

MESH = pl.DeviceIdType.MESH
f32 = jnp.float32
bf16 = jnp.bfloat16


def kernel(
    nodes,
    locals_,
    hidden,
    router,
    chosen,
    w_gate,
    w_up,
    w_down,
    q_lat,
    q_rot,
    cache_lat,
    cache_rot,
    lengths,
    moe_out,
    context,
    rows,
    shares,
    gate_w,
    up_w,
    down_w,
    gate_acc,
    up_acc,
    inner,
    part,
    core_out,
    core_in,
    pair_sum,
    pair_out,
    pair_in,
    line_sum,
    line_out,
    line_in,
    gate_sem,
    up_sem,
    down_sem,
    dz_send,
    dz_recv,
    dy_send,
    dy_recv,
    dc_send,
    dc_recv,
    wz_send,
    wz_recv,
    w_send,
    w_recv,
    rz_send,
    rz_recv,
    ry_send,
    ry_recv,
    rc_send,
    rc_recv,
):
    line = locals_ // PAIR
    core = lax.axis_index("node")
    place = lax.axis_index("local")
    z = place // PAIR
    y = lax.rem(place, PAIR)
    expert = (core * locals_ + place) // (nodes * locals_ // EXPERTS)

    core_peer = {"node": 1 - core, "local": place}
    pair_peer = {"node": core, "local": z * PAIR + 1 - y}

    def ahead(d):
        return lax.rem(z + d, line)

    def line_peer(d):
        return {"node": core, "local": ahead(d) * PAIR + y}

    model_width = hidden.shape[1]
    ck = model_width // NC
    half = ck // 2
    ff = w_gate.shape[1]
    total = nodes * locals_ * 8

    def remote(src, dst, send, recv, peer):
        return pltpu.make_async_remote_copy(
            src_ref=src,
            dst_ref=dst,
            send_sem=send,
            recv_sem=recv,
            device_id=peer,
            device_id_type=MESH,
        )

    def load_gate(k):
        span = pl.ds(pl.multiple_of(k * ck, ck), ck)
        return pltpu.make_async_copy(w_gate.at[span, :], gate_w.at[k], gate_sem.at[k])

    def load_up(k):
        span = pl.ds(pl.multiple_of(k * ck, ck), ck)
        return pltpu.make_async_copy(w_up.at[span, :], up_w.at[k], up_sem.at[k])

    def load_down(k):
        span = pl.ds(pl.multiple_of(k * ck, ck), ck)
        return pltpu.make_async_copy(w_down.at[:, span], down_w.at[k], down_sem.at[k])

    def send_line(k, d):
        block = rows.at[k, core, y, z]
        return remote(block, block, dz_send.at[k, d - 1], dz_recv.at[k, d - 1], line_peer(d))

    def send_pair(k):
        block = rows.at[k, core, y]
        return remote(block, block, dy_send.at[k], dy_recv.at[k], pair_peer)

    def send_core(k):
        block = rows.at[k, core]
        return remote(block, block, dc_send.at[k], dc_recv.at[k], core_peer)

    def share_line(d):
        block = shares.at[core, y, z]
        return remote(block, block, wz_send.at[d - 1], wz_recv.at[d - 1], line_peer(d))

    def share_pair():
        block = shares.at[core, y]
        return remote(block, block, w_send.at[0], w_recv.at[0], pair_peer)

    def share_core():
        block = shares.at[core]
        return remote(block, block, w_send.at[1], w_recv.at[1], core_peer)

    def back_core(t):
        return remote(core_out.at[t], core_in.at[t], rc_send.at[t], rc_recv.at[t], core_peer)

    def back_pair(t):
        return remote(pair_out.at[t], pair_in.at[t], ry_send.at[t], ry_recv.at[t], pair_peer)

    def back_line(t, d):
        return remote(
            line_out.at[t, ahead(d)],
            line_in.at[t, d - 1],
            rz_send.at[t, d - 1],
            rz_recv.at[t, d - 1],
            line_peer(d),
        )

    barrier = pltpu.get_barrier_semaphore()
    peers = [core_peer, pair_peer] + [line_peer(d) for d in range(1, line)]
    for peer in peers:
        pl.semaphore_signal(barrier, inc=1, device_id=peer, device_id_type=MESH)

    for k in range(NC):
        load_gate(k).start()
        load_up(k).start()

    held = hidden[...].astype(f32)
    for k in range(NC):
        both = [held[:, k * ck + h * half : k * ck + (h + 1) * half] for h in range(2)]
        rows[k, core, y, z] = jnp.concatenate(both, axis=0).astype(bf16)

    pl.semaphore_wait(barrier, len(peers))
    for k in range(NC):
        for d in range(1, line):
            send_line(k, d).start()

    scores = jax.nn.sigmoid(jnp.dot(hidden[...], router[...], preferred_element_type=f32))
    slots = lax.broadcasted_iota(jnp.int32, (8, EXPERTS), 1)
    picked = jnp.zeros((8, EXPERTS), f32)
    for j in range(chosen.shape[1]):
        picked = picked + jnp.where(chosen[:, j : j + 1] == slots, scores, 0.0)
    weights = route_scale * picked / jnp.sum(picked, axis=1, keepdims=True)
    shares[core, y, z] = jnp.concatenate([weights, jnp.zeros((8, 128 - EXPERTS), f32)], axis=1)
    for d in range(1, line):
        share_line(d).start()

    gate_acc[...] = jnp.zeros_like(gate_acc)
    up_acc[...] = jnp.zeros_like(up_acc)

    def attend(b):
        logits = lax.dot_general(
            q_lat[b], cache_lat[b], (((1,), (1,)), ((), ())), preferred_element_type=f32
        )
        logits = logits + jnp.dot(q_rot[b], cache_rot[b], preferred_element_type=f32)
        logits = logits * score_scale
        usable = lax.broadcasted_iota(jnp.int32, logits.shape, 1) < lengths[b]
        logits = jnp.where(usable, logits, -1e30)
        raw = jnp.exp(logits - jnp.max(logits, axis=1, keepdims=True))
        probs = (raw / jnp.sum(raw, axis=1, keepdims=True)).astype(bf16)
        context[b] = jnp.dot(probs, cache_lat[b], preferred_element_type=f32).astype(bf16)

    batch = q_lat.shape[0]

    def gather_step(s, carry):
        @pl.when(s < NC)
        def _():
            for d in range(1, line):
                send_line(s, d).wait_recv()
            send_pair(s).start()
            load_down(s).start()

        @pl.when((s >= 1) & (s < NC + 1))
        def _():
            send_pair(s - 1).wait_recv()
            send_core(s - 1).start()

        @pl.when(s < batch)
        def _():
            attend(s)

        @pl.when(s == 3)
        def _():
            for d in range(1, line):
                share_line(d).wait_recv()
            share_pair().start()

        @pl.when(s == 5)
        def _():
            share_pair().wait_recv()
            share_core().start()

        @pl.when(s >= 2)
        def _():
            k = s - 2
            send_core(k).wait_recv()
            load_gate(k).wait()
            load_up(k).wait()
            block = rows[k].astype(f32).reshape(total // 8, 2, 8, half)
            x = jnp.concatenate(
                [block[:, h].reshape(total, half).astype(bf16) for h in range(2)], axis=1
            )
            gate_acc[...] += jnp.dot(x, gate_w[k], preferred_element_type=f32)
            up_acc[...] += jnp.dot(x, up_w[k], preferred_element_type=f32)

        return carry

    lax.fori_loop(0, NC + 2, gather_step, 0)

    gate = gate_acc[...]
    inner[...] = (gate / (1.0 + jnp.exp(-gate)) * up_acc[...]).astype(bf16)
    share_core().wait_recv()
    mine = lax.broadcasted_iota(jnp.int32, (total, 128), 1) == expert
    share = jnp.sum(
        jnp.where(mine, shares[...].reshape(total, 128), 0.0), axis=1, keepdims=True
    )
    gate_acc[...] = jnp.broadcast_to(share, gate_acc.shape)

    def return_step(t, carry):
        @pl.when(t < NC)
        def _():
            load_down(t).wait()
            p = jnp.dot(inner[...], down_w[t], preferred_element_type=f32)
            p = p * gate_acc[:, :1]
            for h in range(2):
                part[t, :, :, :, pl.ds(8 * h, 8), :] = p[:, h * half : (h + 1) * half].reshape(
                    nodes, PAIR, line, 8, half
                )
            core_out[t] = part[t, 1 - core].astype(bf16)
            back_core(t).start()

        @pl.when((t >= 1) & (t < NC + 1))
        def _():
            i = t - 1
            back_core(i).wait_recv()
            pair_sum[i] = part[i, core] + core_in[i].astype(f32)
            pair_out[i] = pair_sum[i, 1 - y].astype(bf16)
            back_pair(i).start()

        @pl.when((t >= 2) & (t < NC + 2))
        def _():
            i = t - 2
            back_pair(i).wait_recv()
            summed = pair_sum[i, y] + pair_in[i].astype(f32)
            line_sum[i] = summed
            line_out[i] = summed.astype(bf16)
            for d in range(1, line):
                back_line(i, d).start()

        @pl.when(t >= 3)
        def _():
            i = t - 3
            summed = line_sum[i, z]
            for d in range(1, line):
                back_line(i, d).wait_recv()
                summed = summed + line_in[i, d - 1].astype(f32)
            both = [summed[8 * h : 8 * h + 8] for h in range(2)]
            span = pl.ds(pl.multiple_of(i * ck, ck), ck)
            moe_out[:, span] = jnp.concatenate(both, axis=1).astype(bf16)

        return carry

    lax.fori_loop(0, NC + 3, return_step, 0)

    def drain(k, carry):
        for d in range(1, line):
            send_line(k, d).wait_send()
            back_line(k, d).wait_send()
        send_pair(k).wait_send()
        send_core(k).wait_send()
        back_pair(k).wait_send()
        back_core(k).wait_send()
        return carry

    lax.fori_loop(0, NC, drain, 0)
    for d in range(1, line):
        share_line(d).wait_send()
    share_pair().wait_send()
    share_core().wait_send()


def fused(
    nodes,
    locals_,
    hidden_rows,
    w_router,
    chosen,
    w_gate,
    w_up,
    w_down,
    q_latent,
    q_rope,
    cache_latent,
    cache_rope,
    lengths,
):
    batch_rows, positions, latent = cache_latent.shape
    rope_width = cache_rope.shape[1]
    heads = q_latent.shape[1] // latent
    row_count, model_width = hidden_rows.shape
    ff = w_gate.shape[1]
    line = locals_ // PAIR
    total = nodes * locals_ * row_count
    ck = model_width // NC
    half = ck // 2
    vmem = pl.BlockSpec(memory_space=pltpu.VMEM)
    hbm = pl.BlockSpec(memory_space=pl.ANY)
    smem = pl.BlockSpec(memory_space=pltpu.SMEM)
    dma = pltpu.SemaphoreType.DMA
    moe_out, context = pl.pallas_call(
        functools.partial(kernel, nodes, locals_),
        out_shape=(
            jax.ShapeDtypeStruct((row_count, model_width), bf16),
            jax.ShapeDtypeStruct((batch_rows, heads, latent), bf16),
        ),
        in_specs=[vmem, vmem, vmem, hbm, hbm, hbm, vmem, vmem, vmem, vmem, smem],
        out_specs=(vmem, vmem),
        scratch_shapes=[
            pltpu.VMEM((NC, nodes, PAIR, line, 16, half), bf16),
            pltpu.VMEM((nodes, PAIR, line, 8, 128), f32),
            pltpu.VMEM((NC, ck, ff), bf16),
            pltpu.VMEM((NC, ck, ff), bf16),
            pltpu.VMEM((NC, ff, ck), bf16),
            pltpu.VMEM((total, ff), f32),
            pltpu.VMEM((total, ff), f32),
            pltpu.VMEM((total, ff), bf16),
            pltpu.VMEM((NC, nodes, PAIR, line, 16, half), f32),
            pltpu.VMEM((NC, PAIR, line, 16, half), bf16),
            pltpu.VMEM((NC, PAIR, line, 16, half), bf16),
            pltpu.VMEM((NC, PAIR, line, 16, half), f32),
            pltpu.VMEM((NC, line, 16, half), bf16),
            pltpu.VMEM((NC, line, 16, half), bf16),
            pltpu.VMEM((NC, line, 16, half), f32),
            pltpu.VMEM((NC, line, 16, half), bf16),
            pltpu.VMEM((NC, line - 1, 16, half), bf16),
            dma((NC,)),
            dma((NC,)),
            dma((NC,)),
            dma((NC, line - 1)),
            dma((NC, line - 1)),
            dma((NC,)),
            dma((NC,)),
            dma((NC,)),
            dma((NC,)),
            dma((line - 1,)),
            dma((line - 1,)),
            dma((2,)),
            dma((2,)),
            dma((NC, line - 1)),
            dma((NC, line - 1)),
            dma((NC,)),
            dma((NC,)),
            dma((NC,)),
            dma((NC,)),
        ],
        compiler_params=pltpu.CompilerParams(
            collective_id=0, has_side_effects=True, vmem_limit_bytes=62 * 1024 * 1024
        ),
    )(
        hidden_rows,
        w_router,
        chosen,
        w_gate,
        w_up,
        w_down,
        q_latent.reshape(batch_rows, heads, latent),
        q_rope.reshape(batch_rows, heads, rope_width),
        cache_latent,
        cache_rope,
        lengths,
    )
    return moe_out, context.reshape(batch_rows, heads * latent)


def solution(mesh):
    nodes, locals_ = mesh.shape["node"], mesh.shape["local"]
    spread = ("rep", "node", "local")
    return jax.shard_map(
        functools.partial(fused, nodes, locals_),
        mesh=mesh,
        in_specs=(
            P(spread, None),
            P(),
            P(spread, None),
            P(None, ("node", "local")),
            P(None, ("node", "local")),
            P(("node", "local"), None),
            P(spread, None),
            P(spread, None),
            P(spread, None, None),
            P(spread, None, None),
            P(spread),
        ),
        out_specs=(P(spread, None), P(spread, None)),
        check_vma=False,
    )
```

```python
import functools

import jax
import jax.numpy as jnp
from jax import lax
from jax.experimental import pallas as pl
from jax.experimental.pallas import tpu as pltpu
from jax.sharding import PartitionSpec as P

EXPERTS = 8
NC = 7
PAIR = 2
LAG = 3

route_scale = 2.5
score_scale = 192.0 ** (-0.5)

MESH = pl.DeviceIdType.MESH
f32 = jnp.float32
bf16 = jnp.bfloat16


def kernel(
    nodes,
    locals_,
    hidden,
    router,
    chosen,
    w_gate,
    w_up,
    w_down,
    q_wide,
    q_rot_wide,
    cache_lat_hbm,
    cache_rot_hbm,
    lengths,
    moe_out,
    context,
    q_lat,
    q_rot,
    cache_lat,
    cache_rot,
    summed_lat,
    rows,
    shares,
    gate_w,
    up_w,
    down_w,
    gate_acc,
    up_acc,
    inner,
    part,
    core_out,
    core_in,
    pair_sum,
    pair_out,
    pair_in,
    line_sum,
    line_out,
    line_in,
    cache_sem,
    gate_sem,
    up_sem,
    down_sem,
    dz_send,
    dz_recv,
    dy_send,
    dy_recv,
    dc_send,
    dc_recv,
    wz_send,
    wz_recv,
    w_send,
    w_recv,
    rz_send,
    rz_recv,
    ry_send,
    ry_recv,
    rc_send,
    rc_recv,
):
    line = locals_ // PAIR
    core = lax.axis_index("node")
    place = lax.axis_index("local")
    z = place // PAIR
    y = lax.rem(place, PAIR)
    expert = (core * locals_ + place) // (nodes * locals_ // EXPERTS)

    core_peer = {"node": 1 - core, "local": place}
    pair_peer = {"node": core, "local": z * PAIR + 1 - y}

    def ahead(d):
        return lax.rem(z + d, line)

    def line_peer(d):
        return {"node": core, "local": ahead(d) * PAIR + y}

    model_width = hidden.shape[1]
    ck = model_width // NC
    half = ck // 2
    ff = w_gate.shape[1]
    total = nodes * locals_ * 8

    def remote(src, dst, send, recv, peer):
        return pltpu.make_async_remote_copy(
            src_ref=src,
            dst_ref=dst,
            send_sem=send,
            recv_sem=recv,
            device_id=peer,
            device_id_type=MESH,
        )

    def load_gate(k):
        span = pl.ds(pl.multiple_of(k * ck, ck), ck)
        return pltpu.make_async_copy(w_gate.at[span, :], gate_w.at[k], gate_sem.at[k])

    def load_up(k):
        span = pl.ds(pl.multiple_of(k * ck, ck), ck)
        return pltpu.make_async_copy(w_up.at[span, :], up_w.at[k], up_sem.at[k])

    def load_down(k):
        span = pl.ds(pl.multiple_of(k * ck, ck), ck)
        return pltpu.make_async_copy(w_down.at[:, span], down_w.at[k], down_sem.at[k])

    def send_line(k, d):
        block = rows.at[k, core, y, z]
        return remote(block, block, dz_send.at[k, d - 1], dz_recv.at[k, d - 1], line_peer(d))

    def send_pair(k):
        block = rows.at[k, core, y]
        return remote(block, block, dy_send.at[k], dy_recv.at[k], pair_peer)

    def send_core(k):
        block = rows.at[k, core]
        return remote(block, block, dc_send.at[k], dc_recv.at[k], core_peer)

    def share_line(d):
        block = shares.at[core, y, z]
        return remote(block, block, wz_send.at[d - 1], wz_recv.at[d - 1], line_peer(d))

    def share_pair():
        block = shares.at[core, y]
        return remote(block, block, w_send.at[0], w_recv.at[0], pair_peer)

    def share_core():
        block = shares.at[core]
        return remote(block, block, w_send.at[1], w_recv.at[1], core_peer)

    def back_core(t):
        return remote(core_out.at[t], core_in.at[t], rc_send.at[t], rc_recv.at[t], core_peer)

    def back_pair(t):
        return remote(pair_out.at[t], pair_in.at[t], ry_send.at[t], ry_recv.at[t], pair_peer)

    def back_line(t, d):
        return remote(
            line_out.at[t, ahead(d)],
            line_in.at[t, d - 1],
            rz_send.at[t, d - 1],
            rz_recv.at[t, d - 1],
            line_peer(d),
        )

    barrier = pltpu.get_barrier_semaphore()
    peers = [core_peer, pair_peer] + [line_peer(d) for d in range(1, line)]
    for peer in peers:
        pl.semaphore_signal(barrier, inc=1, device_id=peer, device_id_type=MESH)

    caches = [
        pltpu.make_async_copy(cache_lat_hbm, cache_lat, cache_sem.at[0]),
        pltpu.make_async_copy(cache_rot_hbm, cache_rot, cache_sem.at[1]),
    ]
    for copy in caches:
        copy.start()
    for k in range(NC):
        load_gate(k).start()
        load_up(k).start()

    held = hidden[...].astype(f32)
    for k in range(NC):
        both = [held[:, k * ck + h * half : k * ck + (h + 1) * half] for h in range(2)]
        rows[k, core, y, z] = jnp.concatenate(both, axis=0).astype(bf16)

    pl.semaphore_wait(barrier, len(peers))
    for k in range(NC):
        for d in range(1, line):
            send_line(k, d).start()

    scores = jax.nn.sigmoid(
        lax.dot_general(
            router[...], hidden[...], (((1,), (1,)), ((), ())), preferred_element_type=f32
        )
    )
    slots = lax.broadcasted_iota(jnp.int32, (EXPERTS, 8), 0)
    picked = jnp.zeros((EXPERTS, 8), f32)
    for j in range(chosen.shape[0]):
        picked = picked + jnp.where(chosen[j : j + 1, :] == slots, scores, 0.0)
    weights = route_scale * picked / jnp.sum(picked, axis=0, keepdims=True)
    weights = jnp.concatenate([weights, jnp.zeros((EXPERTS, 120), f32)], axis=1).T[:8]
    shares[core, y, z] = jnp.concatenate([weights, jnp.zeros((8, 128 - EXPERTS), f32)], axis=1)
    for d in range(1, line):
        share_line(d).start()

    gate_acc[...] = jnp.zeros_like(gate_acc)
    up_acc[...] = jnp.zeros_like(up_acc)

    def attend(b):
        logits = lax.dot_general(
            q_lat[b], cache_lat[b], (((1,), (1,)), ((), ())), preferred_element_type=f32
        )
        logits = logits + jnp.dot(q_rot[b], cache_rot[b], preferred_element_type=f32)
        logits = logits * score_scale
        usable = lax.broadcasted_iota(jnp.int32, logits.shape, 1) < lengths[b]
        logits = jnp.where(usable, logits, -1e30)
        raw = jnp.exp(logits - jnp.max(logits, axis=1, keepdims=True))
        probs = (raw / jnp.sum(raw, axis=1, keepdims=True)).astype(bf16)
        summed_lat[b] = jnp.dot(probs, cache_lat[b], preferred_element_type=f32)

    batch, heads, latent = q_lat.shape
    rope = q_rot.shape[2]

    def spread_queries():
        def group(g, carry):
            first = pl.multiple_of(g * 16, 16)
            lat = q_wide[:, pl.ds(pl.multiple_of(g * 16 * latent, 128), 16 * latent)].astype(f32)
            rot = q_rot_wide[:, pl.ds(pl.multiple_of(g * 16 * rope, 128), 16 * rope)].astype(f32)
            for b in range(batch):
                picks = [lat[b : b + 1, h * latent : (h + 1) * latent] for h in range(16)]
                q_lat[b, pl.ds(first, 16), :] = jnp.concatenate(picks, axis=0).astype(bf16)
                picks = [rot[b : b + 1, h * rope : (h + 1) * rope] for h in range(16)]
                q_rot[b, pl.ds(first, 16), :] = jnp.concatenate(picks, axis=0).astype(bf16)
            return carry

        lax.fori_loop(0, heads // 16, group, 0)

    def join_context():
        def group(g, carry):
            first = pl.multiple_of(g * 8, 8)
            parts = [summed_lat[b, pl.ds(first, 8), :] for b in range(batch)]
            both = [
                jnp.concatenate([v[h : h + 1] for v in parts], axis=0) for h in range(8)
            ]
            span = pl.ds(pl.multiple_of(g * 8 * latent, 128), 8 * latent)
            context[:, span] = jnp.concatenate(both, axis=1).astype(bf16)
            return carry

        lax.fori_loop(0, heads // 8, group, 0)

    def gather_step(s, carry):
        @pl.when(s < NC)
        def _():
            for d in range(1, line):
                send_line(s, d).wait_recv()
            send_pair(s).start()
            load_down(s).start()

        @pl.when((s >= LAG) & (s < NC + LAG))
        def _():
            send_pair(s - LAG).wait_recv()
            send_core(s - LAG).start()

        @pl.when(s == 0)
        def _():
            for copy in caches:
                copy.wait()
            spread_queries()

        @pl.when((s >= 1) & (s <= batch))
        def _():
            attend(s - 1)

        @pl.when(s == batch + 1)
        def _():
            join_context()

        @pl.when(s == 5)
        def _():
            for d in range(1, line):
                share_line(d).wait_recv()
            share_pair().start()

        @pl.when(s == 8)
        def _():
            share_pair().wait_recv()
            share_core().start()

        @pl.when(s > LAG)
        def _():
            k = s - LAG - 1
            send_core(k).wait_recv()
            load_gate(k).wait()
            load_up(k).wait()
            block = rows[k].astype(f32).reshape(total // 8, 2, 8, half)
            x = jnp.concatenate(
                [block[:, h].reshape(total, half).astype(bf16) for h in range(2)], axis=1
            )
            gate_acc[...] += jnp.dot(x, gate_w[k], preferred_element_type=f32)
            up_acc[...] += jnp.dot(x, up_w[k], preferred_element_type=f32)

        return carry

    lax.fori_loop(0, NC + LAG + 1, gather_step, 0)

    gate = gate_acc[...]
    inner[...] = (gate / (1.0 + jnp.exp(-gate)) * up_acc[...]).astype(bf16)
    share_core().wait_recv()
    mine = lax.broadcasted_iota(jnp.int32, (total, 128), 1) == expert
    share = jnp.sum(
        jnp.where(mine, shares[...].reshape(total, 128), 0.0), axis=1, keepdims=True
    )
    gate_acc[...] = jnp.broadcast_to(share, gate_acc.shape)

    def return_step(t, carry):
        @pl.when(t < NC)
        def _():
            load_down(t).wait()
            p = jnp.dot(inner[...], down_w[t], preferred_element_type=f32)
            p = p * gate_acc[:, :1]
            p = p.reshape(nodes, total // nodes, ck)
            keep = jnp.where(core == 0, p[0], p[1])
            give = jnp.where(core == 0, p[1], p[0])
            for h in range(2):
                span = slice(h * half, (h + 1) * half)
                part[t, :, :, pl.ds(8 * h, 8), :] = keep[:, span].reshape(PAIR, line, 8, half)
            give = [give[:, h * half : (h + 1) * half] for h in range(2)]
            give = [v.reshape(PAIR, line, 8, half) for v in give]
            core_out[t] = jnp.concatenate(give, axis=2).astype(bf16)
            back_core(t).start()

        @pl.when((t >= 1) & (t < NC + 1))
        def _():
            i = t - 1
            back_core(i).wait_recv()
            pair_sum[i] = part[i] + core_in[i].astype(f32)
            pair_out[i] = pair_sum[i, 1 - y].astype(bf16)
            back_pair(i).start()

        @pl.when((t >= 1 + LAG) & (t < NC + 1 + LAG))
        def _():
            i = t - 1 - LAG
            back_pair(i).wait_recv()
            summed = pair_sum[i, y] + pair_in[i].astype(f32)
            line_sum[i] = summed
            line_out[i] = summed.astype(bf16)
            for d in range(1, line):
                back_line(i, d).start()

        @pl.when(t >= 1 + 2 * LAG)
        def _():
            i = t - 1 - 2 * LAG
            summed = line_sum[i, z]
            for d in range(1, line):
                back_line(i, d).wait_recv()
                summed = summed + line_in[i, d - 1].astype(f32)
            both = [summed[8 * h : 8 * h + 8] for h in range(2)]
            span = pl.ds(pl.multiple_of(i * ck, ck), ck)
            moe_out[:, span] = jnp.concatenate(both, axis=1).astype(bf16)

        return carry

    lax.fori_loop(0, NC + 1 + 2 * LAG, return_step, 0)

    def drain(k, carry):
        for d in range(1, line):
            send_line(k, d).wait_send()
            back_line(k, d).wait_send()
        send_pair(k).wait_send()
        send_core(k).wait_send()
        back_pair(k).wait_send()
        back_core(k).wait_send()
        return carry

    lax.fori_loop(0, NC, drain, 0)
    for d in range(1, line):
        share_line(d).wait_send()
    share_pair().wait_send()
    share_core().wait_send()


def fused(
    nodes,
    locals_,
    hidden_rows,
    w_router,
    chosen,
    w_gate,
    w_up,
    w_down,
    q_latent,
    q_rope,
    cache_latent,
    cache_rope,
    lengths,
):
    batch_rows, positions, latent = cache_latent.shape
    rope_width = cache_rope.shape[1]
    heads = q_latent.shape[1] // latent
    row_count, model_width = hidden_rows.shape
    ff = w_gate.shape[1]
    line = locals_ // PAIR
    total = nodes * locals_ * row_count
    ck = model_width // NC
    half = ck // 2
    vmem = pl.BlockSpec(memory_space=pltpu.VMEM)
    hbm = pl.BlockSpec(memory_space=pl.ANY)
    smem = pl.BlockSpec(memory_space=pltpu.SMEM)
    dma = pltpu.SemaphoreType.DMA
    moe_out, context = pl.pallas_call(
        functools.partial(kernel, nodes, locals_),
        out_shape=(
            jax.ShapeDtypeStruct((row_count, model_width), bf16),
            jax.ShapeDtypeStruct((batch_rows, heads * latent), bf16),
        ),
        in_specs=[vmem, vmem, vmem, hbm, hbm, hbm, vmem, vmem, hbm, hbm, smem],
        out_specs=(vmem, vmem),
        scratch_shapes=[
            pltpu.VMEM((batch_rows, heads, latent), bf16),
            pltpu.VMEM((batch_rows, heads, rope_width), bf16),
            pltpu.VMEM(cache_latent.shape, bf16),
            pltpu.VMEM(cache_rope.shape, bf16),
            pltpu.VMEM((batch_rows, heads, latent), f32),
            pltpu.VMEM((NC, nodes, PAIR, line, 16, half), bf16),
            pltpu.VMEM((nodes, PAIR, line, 8, 128), f32),
            pltpu.VMEM((NC, ck, ff), bf16),
            pltpu.VMEM((NC, ck, ff), bf16),
            pltpu.VMEM((NC, ff, ck), bf16),
            pltpu.VMEM((total, ff), f32),
            pltpu.VMEM((total, ff), f32),
            pltpu.VMEM((total, ff), bf16),
            pltpu.VMEM((NC, PAIR, line, 16, half), f32),
            pltpu.VMEM((NC, PAIR, line, 16, half), bf16),
            pltpu.VMEM((NC, PAIR, line, 16, half), bf16),
            pltpu.VMEM((NC, PAIR, line, 16, half), f32),
            pltpu.VMEM((NC, line, 16, half), bf16),
            pltpu.VMEM((NC, line, 16, half), bf16),
            pltpu.VMEM((NC, line, 16, half), f32),
            pltpu.VMEM((NC, line, 16, half), bf16),
            pltpu.VMEM((NC, line - 1, 16, half), bf16),
            dma((2,)),
            dma((NC,)),
            dma((NC,)),
            dma((NC,)),
            dma((NC, line - 1)),
            dma((NC, line - 1)),
            dma((NC,)),
            dma((NC,)),
            dma((NC,)),
            dma((NC,)),
            dma((line - 1,)),
            dma((line - 1,)),
            dma((2,)),
            dma((2,)),
            dma((NC, line - 1)),
            dma((NC, line - 1)),
            dma((NC,)),
            dma((NC,)),
            dma((NC,)),
            dma((NC,)),
        ],
        compiler_params=pltpu.CompilerParams(
            collective_id=0, has_side_effects=True, vmem_limit_bytes=62 * 1024 * 1024
        ),
    )(
        hidden_rows,
        w_router.T,
        chosen.T,
        w_gate,
        w_up,
        w_down,
        q_latent,
        q_rope,
        cache_latent,
        cache_rope,
        lengths,
    )
    return moe_out, context


def solution(mesh):
    nodes, locals_ = mesh.shape["node"], mesh.shape["local"]
    spread = ("rep", "node", "local")
    return jax.shard_map(
        functools.partial(fused, nodes, locals_),
        mesh=mesh,
        in_specs=(
            P(spread, None),
            P(),
            P(spread, None),
            P(None, ("node", "local")),
            P(None, ("node", "local")),
            P(("node", "local"), None),
            P(spread, None),
            P(spread, None),
            P(spread, None, None),
            P(spread, None, None),
            P(spread),
        ),
        out_specs=(P(spread, None), P(spread, None)),
        check_vma=False,
    )
```

```python
import functools

import jax
import jax.numpy as jnp
from jax import lax
from jax.experimental import pallas as pl
from jax.experimental.pallas import tpu as pltpu
from jax.sharding import PartitionSpec as P

EXPERTS = 8
NC = 7
PAIR = 2
LAG = 3
CORE_LAG = 1
BACK_CORE = 1
BACK_LAG = 3

route_scale = 2.5
score_scale = 192.0 ** (-0.5)

MESH = pl.DeviceIdType.MESH
f32 = jnp.float32
bf16 = jnp.bfloat16


def kernel(
    nodes,
    locals_,
    hidden,
    router,
    chosen,
    w_gate,
    w_up,
    w_down,
    q_wide,
    q_rot_wide,
    cache_lat_hbm,
    cache_rot_hbm,
    lengths,
    moe_out,
    context,
    q_lat,
    q_rot,
    cache_lat,
    cache_rot,
    summed_lat,
    rows,
    shares,
    gate_w,
    up_w,
    down_w,
    gate_acc,
    up_acc,
    inner,
    part,
    core_out,
    core_in,
    pair_sum,
    pair_out,
    pair_in,
    line_sum,
    line_out,
    line_in,
    cache_sem,
    gate_sem,
    up_sem,
    down_sem,
    dz_send,
    dz_recv,
    dy_send,
    dy_recv,
    dc_send,
    dc_recv,
    wz_send,
    wz_recv,
    w_send,
    w_recv,
    rz_send,
    rz_recv,
    ry_send,
    ry_recv,
    rc_send,
    rc_recv,
):
    line = locals_ // PAIR
    core = lax.axis_index("node")
    place = lax.axis_index("local")
    z = place // PAIR
    y = lax.rem(place, PAIR)
    expert = (core * locals_ + place) // (nodes * locals_ // EXPERTS)

    core_peer = {"node": 1 - core, "local": place}
    pair_peer = {"node": core, "local": z * PAIR + 1 - y}

    def ahead(d):
        return lax.rem(z + d, line)

    def line_peer(d):
        return {"node": core, "local": ahead(d) * PAIR + y}

    model_width = hidden.shape[1]
    ck = model_width // NC
    half = ck // 2
    ff = w_gate.shape[1]
    total = nodes * locals_ * 8

    def remote(src, dst, send, recv, peer):
        return pltpu.make_async_remote_copy(
            src_ref=src,
            dst_ref=dst,
            send_sem=send,
            recv_sem=recv,
            device_id=peer,
            device_id_type=MESH,
        )

    def load_gate(k):
        span = pl.ds(pl.multiple_of(k * ck, ck), ck)
        return pltpu.make_async_copy(w_gate.at[span, :], gate_w.at[k], gate_sem.at[k])

    def load_up(k):
        span = pl.ds(pl.multiple_of(k * ck, ck), ck)
        return pltpu.make_async_copy(w_up.at[span, :], up_w.at[k], up_sem.at[k])

    def load_down(k):
        span = pl.ds(pl.multiple_of(k * ck, ck), ck)
        return pltpu.make_async_copy(w_down.at[:, span], down_w.at[k], down_sem.at[k])

    def send_line(k, d):
        block = rows.at[k, core, y, z]
        return remote(block, block, dz_send.at[k, d - 1], dz_recv.at[k, d - 1], line_peer(d))

    def send_pair(k):
        block = rows.at[k, core, y]
        return remote(block, block, dy_send.at[k], dy_recv.at[k], pair_peer)

    def send_core(k):
        block = rows.at[k, core]
        return remote(block, block, dc_send.at[k], dc_recv.at[k], core_peer)

    def share_line(d):
        block = shares.at[core, y, z]
        return remote(block, block, wz_send.at[d - 1], wz_recv.at[d - 1], line_peer(d))

    def share_pair():
        block = shares.at[core, y]
        return remote(block, block, w_send.at[0], w_recv.at[0], pair_peer)

    def share_core():
        block = shares.at[core]
        return remote(block, block, w_send.at[1], w_recv.at[1], core_peer)

    def back_core(t):
        return remote(core_out.at[t], core_in.at[t], rc_send.at[t], rc_recv.at[t], core_peer)

    def back_pair(t):
        return remote(pair_out.at[t], pair_in.at[t], ry_send.at[t], ry_recv.at[t], pair_peer)

    def back_line(t, d):
        return remote(
            line_out.at[t, ahead(d)],
            line_in.at[t, d - 1],
            rz_send.at[t, d - 1],
            rz_recv.at[t, d - 1],
            line_peer(d),
        )

    barrier = pltpu.get_barrier_semaphore()
    peers = [core_peer, pair_peer] + [line_peer(d) for d in range(1, line)]
    for peer in peers:
        pl.semaphore_signal(barrier, inc=1, device_id=peer, device_id_type=MESH)

    caches = [
        pltpu.make_async_copy(cache_lat_hbm, cache_lat, cache_sem.at[0]),
        pltpu.make_async_copy(cache_rot_hbm, cache_rot, cache_sem.at[1]),
    ]
    for copy in caches:
        copy.start()
    for k in range(NC):
        load_gate(k).start()
        load_up(k).start()

    held = hidden[...].astype(f32)
    for k in range(NC):
        both = [held[:, k * ck + h * half : k * ck + (h + 1) * half] for h in range(2)]
        rows[k, core, y, z] = jnp.concatenate(both, axis=0).astype(bf16)

    pl.semaphore_wait(barrier, len(peers))
    for k in range(NC):
        for d in range(1, line):
            send_line(k, d).start()

    scores = jax.nn.sigmoid(
        lax.dot_general(
            router[...], hidden[...], (((1,), (1,)), ((), ())), preferred_element_type=f32
        )
    )
    slots = lax.broadcasted_iota(jnp.int32, (EXPERTS, 8), 0)
    picked = jnp.zeros((EXPERTS, 8), f32)
    for j in range(chosen.shape[0]):
        picked = picked + jnp.where(chosen[j : j + 1, :] == slots, scores, 0.0)
    weights = route_scale * picked / jnp.sum(picked, axis=0, keepdims=True)
    weights = jnp.concatenate([weights, jnp.zeros((EXPERTS, 120), f32)], axis=1).T[:8]
    shares[core, y, z] = jnp.concatenate([weights, jnp.zeros((8, 128 - EXPERTS), f32)], axis=1)
    for d in range(1, line):
        share_line(d).start()

    gate_acc[...] = jnp.zeros_like(gate_acc)
    up_acc[...] = jnp.zeros_like(up_acc)

    def attend(b):
        logits = lax.dot_general(
            q_lat[b], cache_lat[b], (((1,), (1,)), ((), ())), preferred_element_type=f32
        )
        logits = logits + jnp.dot(q_rot[b], cache_rot[b], preferred_element_type=f32)
        logits = logits * score_scale
        usable = lax.broadcasted_iota(jnp.int32, logits.shape, 1) < lengths[b]
        logits = jnp.where(usable, logits, -1e30)
        raw = jnp.exp(logits - jnp.max(logits, axis=1, keepdims=True))
        probs = (raw / jnp.sum(raw, axis=1, keepdims=True)).astype(bf16)
        summed_lat[b] = jnp.dot(probs, cache_lat[b], preferred_element_type=f32)

    batch, heads, latent = q_lat.shape
    rope = q_rot.shape[2]

    def spread_queries():
        def group(g, carry):
            first = pl.multiple_of(g * 16, 16)
            lat = q_wide[:, pl.ds(pl.multiple_of(g * 16 * latent, 128), 16 * latent)].astype(f32)
            rot = q_rot_wide[:, pl.ds(pl.multiple_of(g * 16 * rope, 128), 16 * rope)].astype(f32)
            for b in range(batch):
                picks = [lat[b : b + 1, h * latent : (h + 1) * latent] for h in range(16)]
                q_lat[b, pl.ds(first, 16), :] = jnp.concatenate(picks, axis=0).astype(bf16)
                picks = [rot[b : b + 1, h * rope : (h + 1) * rope] for h in range(16)]
                q_rot[b, pl.ds(first, 16), :] = jnp.concatenate(picks, axis=0).astype(bf16)
            return carry

        lax.fori_loop(0, heads // 16, group, 0)

    def join_context():
        def group(g, carry):
            first = pl.multiple_of(g * 8, 8)
            parts = [summed_lat[b, pl.ds(first, 8), :] for b in range(batch)]
            both = [
                jnp.concatenate([v[h : h + 1] for v in parts], axis=0) for h in range(8)
            ]
            span = pl.ds(pl.multiple_of(g * 8 * latent, 128), 8 * latent)
            context[:, span] = jnp.concatenate(both, axis=1).astype(bf16)
            return carry

        lax.fori_loop(0, heads // 8, group, 0)

    def gather_step(s, carry):
        @pl.when(s < NC)
        def _():
            for d in range(1, line):
                send_line(s, d).wait_recv()
            send_pair(s).start()
            load_down(s).start()

        @pl.when((s >= LAG) & (s < NC + LAG))
        def _():
            send_pair(s - LAG).wait_recv()
            send_core(s - LAG).start()

        @pl.when(s == 0)
        def _():
            for copy in caches:
                copy.wait()
            spread_queries()

        @pl.when((s >= 1) & (s <= batch))
        def _():
            attend(s - 1)

        @pl.when(s == batch + 1)
        def _():
            join_context()

        @pl.when(s == 5)
        def _():
            for d in range(1, line):
                share_line(d).wait_recv()
            share_pair().start()

        @pl.when(s == 8)
        def _():
            share_pair().wait_recv()
            share_core().start()

        @pl.when(s >= LAG + CORE_LAG)
        def _():
            k = s - LAG - CORE_LAG
            send_core(k).wait_recv()
            load_gate(k).wait()
            load_up(k).wait()
            block = rows[k].astype(f32).reshape(total // 8, 2, 8, half)
            x = jnp.concatenate(
                [block[:, h].reshape(total, half).astype(bf16) for h in range(2)], axis=1
            )
            gate_acc[...] += jnp.dot(x, gate_w[k], preferred_element_type=f32)
            up_acc[...] += jnp.dot(x, up_w[k], preferred_element_type=f32)

        return carry

    lax.fori_loop(0, NC + LAG + CORE_LAG, gather_step, 0)

    gate = gate_acc[...]
    inner[...] = (gate / (1.0 + jnp.exp(-gate)) * up_acc[...]).astype(bf16)
    share_core().wait_recv()
    mine = lax.broadcasted_iota(jnp.int32, (total, 128), 1) == expert
    share = jnp.sum(
        jnp.where(mine, shares[...].reshape(total, 128), 0.0), axis=1, keepdims=True
    )
    gate_acc[...] = jnp.broadcast_to(share, gate_acc.shape)

    def return_step(t, carry):
        @pl.when(t < NC)
        def _():
            load_down(t).wait()
            p = jnp.dot(inner[...], down_w[t], preferred_element_type=f32)
            p = p * gate_acc[:, :1]
            p = p.reshape(nodes, total // nodes, ck)
            keep = jnp.where(core == 0, p[0], p[1])
            give = jnp.where(core == 0, p[1], p[0])
            for h in range(2):
                span = slice(h * half, (h + 1) * half)
                part[t, :, :, pl.ds(8 * h, 8), :] = keep[:, span].reshape(PAIR, line, 8, half)
            give = [give[:, h * half : (h + 1) * half] for h in range(2)]
            give = [v.reshape(PAIR, line, 8, half) for v in give]
            core_out[t] = jnp.concatenate(give, axis=2).astype(bf16)
            back_core(t).start()

        @pl.when((t >= BACK_CORE) & (t < NC + BACK_CORE))
        def _():
            i = t - BACK_CORE
            back_core(i).wait_recv()
            pair_sum[i] = part[i] + core_in[i].astype(f32)
            pair_out[i] = pair_sum[i, 1 - y].astype(bf16)
            back_pair(i).start()

        @pl.when((t >= BACK_CORE + BACK_LAG) & (t < NC + BACK_CORE + BACK_LAG))
        def _():
            i = t - BACK_CORE - BACK_LAG
            back_pair(i).wait_recv()
            summed = pair_sum[i, y] + pair_in[i].astype(f32)
            line_sum[i] = summed
            line_out[i] = summed.astype(bf16)
            for d in range(1, line):
                back_line(i, d).start()

        @pl.when(t >= BACK_CORE + 2 * BACK_LAG)
        def _():
            i = t - BACK_CORE - 2 * BACK_LAG
            summed = line_sum[i, z]
            for d in range(1, line):
                back_line(i, d).wait_recv()
                summed = summed + line_in[i, d - 1].astype(f32)
            both = [summed[8 * h : 8 * h + 8] for h in range(2)]
            span = pl.ds(pl.multiple_of(i * ck, ck), ck)
            moe_out[:, span] = jnp.concatenate(both, axis=1).astype(bf16)

        return carry

    lax.fori_loop(0, NC + BACK_CORE + 2 * BACK_LAG, return_step, 0)

    def drain(k, carry):
        for d in range(1, line):
            send_line(k, d).wait_send()
            back_line(k, d).wait_send()
        send_pair(k).wait_send()
        send_core(k).wait_send()
        back_pair(k).wait_send()
        back_core(k).wait_send()
        return carry

    lax.fori_loop(0, NC, drain, 0)
    for d in range(1, line):
        share_line(d).wait_send()
    share_pair().wait_send()
    share_core().wait_send()


def place_outputs(moe, context, moe_out, context_out, sems):
    copies = [
        pltpu.make_async_copy(moe, moe_out, sems.at[0]),
        pltpu.make_async_copy(context, context_out, sems.at[1]),
    ]
    for copy in copies:
        copy.start()
    for copy in copies:
        copy.wait()


def fused(
    nodes,
    locals_,
    hidden_rows,
    w_router,
    chosen,
    w_gate,
    w_up,
    w_down,
    q_latent,
    q_rope,
    cache_latent,
    cache_rope,
    lengths,
):
    batch_rows, positions, latent = cache_latent.shape
    rope_width = cache_rope.shape[1]
    heads = q_latent.shape[1] // latent
    row_count, model_width = hidden_rows.shape
    ff = w_gate.shape[1]
    line = locals_ // PAIR
    total = nodes * locals_ * row_count
    ck = model_width // NC
    half = ck // 2
    vmem = pl.BlockSpec(memory_space=pltpu.VMEM)
    hbm = pl.BlockSpec(memory_space=pl.ANY)
    smem = pl.BlockSpec(memory_space=pltpu.SMEM)
    dma = pltpu.SemaphoreType.DMA
    moe_out, context = pl.pallas_call(
        functools.partial(kernel, nodes, locals_),
        out_shape=(
            jax.ShapeDtypeStruct((row_count, model_width), bf16),
            jax.ShapeDtypeStruct((batch_rows, heads * latent), bf16),
        ),
        in_specs=[vmem, vmem, vmem, hbm, hbm, hbm, vmem, vmem, hbm, hbm, smem],
        out_specs=(vmem, vmem),
        scratch_shapes=[
            pltpu.VMEM((batch_rows, heads, latent), bf16),
            pltpu.VMEM((batch_rows, heads, rope_width), bf16),
            pltpu.VMEM(cache_latent.shape, bf16),
            pltpu.VMEM(cache_rope.shape, bf16),
            pltpu.VMEM((batch_rows, heads, latent), f32),
            pltpu.VMEM((NC, nodes, PAIR, line, 16, half), bf16),
            pltpu.VMEM((nodes, PAIR, line, 8, 128), f32),
            pltpu.VMEM((NC, ck, ff), bf16),
            pltpu.VMEM((NC, ck, ff), bf16),
            pltpu.VMEM((NC, ff, ck), bf16),
            pltpu.VMEM((total, ff), f32),
            pltpu.VMEM((total, ff), f32),
            pltpu.VMEM((total, ff), bf16),
            pltpu.VMEM((NC, PAIR, line, 16, half), f32),
            pltpu.VMEM((NC, PAIR, line, 16, half), bf16),
            pltpu.VMEM((NC, PAIR, line, 16, half), bf16),
            pltpu.VMEM((NC, PAIR, line, 16, half), f32),
            pltpu.VMEM((NC, line, 16, half), bf16),
            pltpu.VMEM((NC, line, 16, half), bf16),
            pltpu.VMEM((NC, line, 16, half), f32),
            pltpu.VMEM((NC, line, 16, half), bf16),
            pltpu.VMEM((NC, line - 1, 16, half), bf16),
            dma((2,)),
            dma((NC,)),
            dma((NC,)),
            dma((NC,)),
            dma((NC, line - 1)),
            dma((NC, line - 1)),
            dma((NC,)),
            dma((NC,)),
            dma((NC,)),
            dma((NC,)),
            dma((line - 1,)),
            dma((line - 1,)),
            dma((2,)),
            dma((2,)),
            dma((NC, line - 1)),
            dma((NC, line - 1)),
            dma((NC,)),
            dma((NC,)),
            dma((NC,)),
            dma((NC,)),
        ],
        compiler_params=pltpu.CompilerParams(
            collective_id=0, has_side_effects=True, vmem_limit_bytes=62 * 1024 * 1024
        ),
    )(
        hidden_rows,
        w_router.T,
        chosen.T,
        w_gate,
        w_up,
        w_down,
        q_latent,
        q_rope,
        cache_latent,
        cache_rope,
        lengths,
    )
    return pl.pallas_call(
        place_outputs,
        out_shape=(
            jax.ShapeDtypeStruct(moe_out.shape, bf16),
            jax.ShapeDtypeStruct(context.shape, bf16),
        ),
        in_specs=[hbm, hbm],
        out_specs=(vmem, vmem),
        scratch_shapes=[dma((2,))],
    )(moe_out, context)


def solution(mesh):
    nodes, locals_ = mesh.shape["node"], mesh.shape["local"]
    spread = ("rep", "node", "local")
    return jax.shard_map(
        functools.partial(fused, nodes, locals_),
        mesh=mesh,
        in_specs=(
            P(spread, None),
            P(),
            P(spread, None),
            P(None, ("node", "local")),
            P(None, ("node", "local")),
            P(("node", "local"), None),
            P(spread, None),
            P(spread, None),
            P(spread, None, None),
            P(spread, None, None),
            P(spread),
        ),
        out_specs=(P(spread, None), P(spread, None)),
        check_vma=False,
    )
```

```python
import functools

import jax
import jax.numpy as jnp
from jax import lax
from jax.experimental import pallas as pl
from jax.experimental.pallas import tpu as pltpu
from jax.sharding import PartitionSpec as P

EXPERTS = 8
NC = 7
PAIR = 2
LAG = 3
CORE_LAG = 1
BACK_CORE = 1
BACK_LAG = 3

route_scale = 2.5
score_scale = 192.0 ** (-0.5)

MESH = pl.DeviceIdType.MESH
f32 = jnp.float32
bf16 = jnp.bfloat16


def kernel(
    nodes,
    locals_,
    hidden,
    router,
    chosen,
    w_gate,
    w_up,
    w_down,
    q_wide,
    q_rot_wide,
    cache_lat_hbm,
    cache_rot_hbm,
    lengths,
    moe_out,
    context,
    q_lat,
    q_rot,
    cache_lat,
    cache_rot,
    summed_lat,
    rows,
    shares,
    gate_w,
    up_w,
    down_w,
    gate_acc,
    up_acc,
    inner,
    part,
    core_out,
    core_in,
    pair_sum,
    pair_out,
    pair_in,
    line_sum,
    line_out,
    line_in,
    cache_sem,
    gate_sem,
    up_sem,
    down_sem,
    dz_send,
    dz_recv,
    dy_send,
    dy_recv,
    dc_send,
    dc_recv,
    wz_send,
    wz_recv,
    w_send,
    w_recv,
    rz_send,
    rz_recv,
    ry_send,
    ry_recv,
    rc_send,
    rc_recv,
):
    line = locals_ // PAIR
    core = lax.axis_index("node")
    place = lax.axis_index("local")
    z = place // PAIR
    y = lax.rem(place, PAIR)
    expert = (core * locals_ + place) // (nodes * locals_ // EXPERTS)

    core_peer = {"node": 1 - core, "local": place}
    pair_peer = {"node": core, "local": z * PAIR + 1 - y}

    def ahead(d):
        return lax.rem(z + d, line)

    def line_peer(d):
        return {"node": core, "local": ahead(d) * PAIR + y}

    model_width = hidden.shape[1]
    ck = model_width // NC
    half = ck // 2
    ff = w_gate.shape[1]
    total = nodes * locals_ * 8

    def remote(src, dst, send, recv, peer):
        return pltpu.make_async_remote_copy(
            src_ref=src,
            dst_ref=dst,
            send_sem=send,
            recv_sem=recv,
            device_id=peer,
            device_id_type=MESH,
        )

    def load_gate(k):
        span = pl.ds(pl.multiple_of(k * ck, ck), ck)
        return pltpu.make_async_copy(w_gate.at[span, :], gate_w.at[k], gate_sem.at[k])

    def load_up(k):
        span = pl.ds(pl.multiple_of(k * ck, ck), ck)
        return pltpu.make_async_copy(w_up.at[span, :], up_w.at[k], up_sem.at[k])

    def load_down(k):
        span = pl.ds(pl.multiple_of(k * ck, ck), ck)
        return pltpu.make_async_copy(w_down.at[:, span], down_w.at[k], down_sem.at[k])

    def send_line(k, d):
        block = rows.at[k, core, y, z]
        return remote(block, block, dz_send.at[k, d - 1], dz_recv.at[k, d - 1], line_peer(d))

    def send_pair(k):
        block = rows.at[k, core, y]
        return remote(block, block, dy_send.at[k], dy_recv.at[k], pair_peer)

    def send_core(k):
        block = rows.at[k, core]
        return remote(block, block, dc_send.at[k], dc_recv.at[k], core_peer)

    def share_line(d):
        block = shares.at[core, y, z]
        return remote(block, block, wz_send.at[d - 1], wz_recv.at[d - 1], line_peer(d))

    def share_pair():
        block = shares.at[core, y]
        return remote(block, block, w_send.at[0], w_recv.at[0], pair_peer)

    def share_core():
        block = shares.at[core]
        return remote(block, block, w_send.at[1], w_recv.at[1], core_peer)

    def back_core(t):
        return remote(core_out.at[t], core_in.at[t], rc_send.at[t], rc_recv.at[t], core_peer)

    def back_pair(t):
        return remote(pair_out.at[t], pair_in.at[t], ry_send.at[t], ry_recv.at[t], pair_peer)

    def back_line(t, d):
        return remote(
            line_out.at[t, ahead(d)],
            line_in.at[t, d - 1],
            rz_send.at[t, d - 1],
            rz_recv.at[t, d - 1],
            line_peer(d),
        )

    barrier = pltpu.get_barrier_semaphore()
    peers = [core_peer, pair_peer] + [line_peer(d) for d in range(1, line)]
    for peer in peers:
        pl.semaphore_signal(barrier, inc=1, device_id=peer, device_id_type=MESH)

    caches = [
        pltpu.make_async_copy(cache_lat_hbm, cache_lat, cache_sem.at[0]),
        pltpu.make_async_copy(cache_rot_hbm, cache_rot, cache_sem.at[1]),
    ]
    for copy in caches:
        copy.start()

    held = hidden[...].astype(f32)
    for k in range(NC):
        both = [held[:, k * ck + h * half : k * ck + (h + 1) * half] for h in range(2)]
        rows[k, core, y, z] = jnp.concatenate(both, axis=0).astype(bf16)

    pl.semaphore_wait(barrier, len(peers))
    for k in range(NC):
        for d in range(1, line):
            send_line(k, d).start()
    for k in range(NC):
        load_gate(k).start()
        load_up(k).start()

    scores = jax.nn.sigmoid(
        lax.dot_general(
            router[...], hidden[...], (((1,), (1,)), ((), ())), preferred_element_type=f32
        )
    )
    slots = lax.broadcasted_iota(jnp.int32, (EXPERTS, 8), 0)
    picked = jnp.zeros((EXPERTS, 8), f32)
    for j in range(chosen.shape[0]):
        picked = picked + jnp.where(chosen[j : j + 1, :] == slots, scores, 0.0)
    weights = route_scale * picked / jnp.sum(picked, axis=0, keepdims=True)
    weights = jnp.concatenate([weights, jnp.zeros((EXPERTS, 120), f32)], axis=1).T[:8]
    shares[core, y, z] = jnp.concatenate([weights, jnp.zeros((8, 128 - EXPERTS), f32)], axis=1)
    for d in range(1, line):
        share_line(d).start()

    gate_acc[...] = jnp.zeros_like(gate_acc)
    up_acc[...] = jnp.zeros_like(up_acc)

    def attend(b):
        logits = lax.dot_general(
            q_lat[b], cache_lat[b], (((1,), (1,)), ((), ())), preferred_element_type=f32
        )
        logits = logits + jnp.dot(q_rot[b], cache_rot[b], preferred_element_type=f32)
        logits = logits * score_scale
        usable = lax.broadcasted_iota(jnp.int32, logits.shape, 1) < lengths[b]
        logits = jnp.where(usable, logits, -1e30)
        raw = jnp.exp(logits - jnp.max(logits, axis=1, keepdims=True))
        probs = (raw / jnp.sum(raw, axis=1, keepdims=True)).astype(bf16)
        summed_lat[b] = jnp.dot(probs, cache_lat[b], preferred_element_type=f32)

    batch, heads, latent = q_lat.shape
    rope = q_rot.shape[2]

    def spread_queries():
        def group(g, carry):
            first = pl.multiple_of(g * 16, 16)
            lat = q_wide[:, pl.ds(pl.multiple_of(g * 16 * latent, 128), 16 * latent)].astype(f32)
            rot = q_rot_wide[:, pl.ds(pl.multiple_of(g * 16 * rope, 128), 16 * rope)].astype(f32)
            for b in range(batch):
                picks = [lat[b : b + 1, h * latent : (h + 1) * latent] for h in range(16)]
                q_lat[b, pl.ds(first, 16), :] = jnp.concatenate(picks, axis=0).astype(bf16)
                picks = [rot[b : b + 1, h * rope : (h + 1) * rope] for h in range(16)]
                q_rot[b, pl.ds(first, 16), :] = jnp.concatenate(picks, axis=0).astype(bf16)
            return carry

        lax.fori_loop(0, heads // 16, group, 0)

    def join_context():
        def group(g, carry):
            first = pl.multiple_of(g * 8, 8)
            parts = [summed_lat[b, pl.ds(first, 8), :] for b in range(batch)]
            both = [
                jnp.concatenate([v[h : h + 1] for v in parts], axis=0) for h in range(8)
            ]
            span = pl.ds(pl.multiple_of(g * 8 * latent, 128), 8 * latent)
            context[:, span] = jnp.concatenate(both, axis=1).astype(bf16)
            return carry

        lax.fori_loop(0, heads // 8, group, 0)

    def gather_step(s, carry):
        @pl.when(s < NC)
        def _():
            for d in range(1, line):
                send_line(s, d).wait_recv()
            send_pair(s).start()
            load_down(s).start()

        @pl.when((s >= LAG) & (s < NC + LAG))
        def _():
            send_pair(s - LAG).wait_recv()
            send_core(s - LAG).start()

        @pl.when(s == 0)
        def _():
            for copy in caches:
                copy.wait()
            spread_queries()

        @pl.when((s >= 1) & (s <= batch))
        def _():
            attend(s - 1)

        @pl.when(s == batch + 1)
        def _():
            join_context()

        @pl.when(s == 5)
        def _():
            for d in range(1, line):
                share_line(d).wait_recv()
            share_pair().start()

        @pl.when(s == 8)
        def _():
            share_pair().wait_recv()
            share_core().start()

        @pl.when(s >= LAG + CORE_LAG)
        def _():
            k = s - LAG - CORE_LAG
            send_core(k).wait_recv()
            load_gate(k).wait()
            load_up(k).wait()
            block = rows[k].astype(f32).reshape(total // 8, 2, 8, half)
            x = jnp.concatenate(
                [block[:, h].reshape(total, half).astype(bf16) for h in range(2)], axis=1
            )
            gate_acc[...] += jnp.dot(x, gate_w[k], preferred_element_type=f32)
            up_acc[...] += jnp.dot(x, up_w[k], preferred_element_type=f32)

        return carry

    lax.fori_loop(0, NC + LAG + CORE_LAG, gather_step, 0)

    gate = gate_acc[...]
    inner[...] = (gate / (1.0 + jnp.exp(-gate)) * up_acc[...]).astype(bf16)
    share_core().wait_recv()
    mine = lax.broadcasted_iota(jnp.int32, (total, 128), 1) == expert
    share = jnp.sum(
        jnp.where(mine, shares[...].reshape(total, 128), 0.0), axis=1, keepdims=True
    )
    gate_acc[...] = jnp.broadcast_to(share, gate_acc.shape)

    def return_step(t, carry):
        @pl.when(t < NC)
        def _():
            load_down(t).wait()
            p = jnp.dot(inner[...], down_w[t], preferred_element_type=f32)
            p = p * gate_acc[:, :1]
            p = p.reshape(nodes, total // nodes, ck)
            keep = jnp.where(core == 0, p[0], p[1])
            give = jnp.where(core == 0, p[1], p[0])
            for h in range(2):
                span = slice(h * half, (h + 1) * half)
                part[t, :, :, pl.ds(8 * h, 8), :] = keep[:, span].reshape(PAIR, line, 8, half)
            give = [give[:, h * half : (h + 1) * half] for h in range(2)]
            give = [v.reshape(PAIR, line, 8, half) for v in give]
            core_out[t] = jnp.concatenate(give, axis=2).astype(bf16)
            back_core(t).start()

        @pl.when((t >= BACK_CORE) & (t < NC + BACK_CORE))
        def _():
            i = t - BACK_CORE
            back_core(i).wait_recv()
            pair_sum[i] = part[i] + core_in[i].astype(f32)
            pair_out[i] = pair_sum[i, 1 - y].astype(bf16)
            back_pair(i).start()

        @pl.when((t >= BACK_CORE + BACK_LAG) & (t < NC + BACK_CORE + BACK_LAG))
        def _():
            i = t - BACK_CORE - BACK_LAG
            back_pair(i).wait_recv()
            summed = pair_sum[i, y] + pair_in[i].astype(f32)
            line_sum[i] = summed
            line_out[i] = summed.astype(bf16)
            for d in range(1, line):
                back_line(i, d).start()

        @pl.when(t >= BACK_CORE + 2 * BACK_LAG)
        def _():
            i = t - BACK_CORE - 2 * BACK_LAG
            summed = line_sum[i, z]
            for d in range(1, line):
                back_line(i, d).wait_recv()
                summed = summed + line_in[i, d - 1].astype(f32)
            both = [summed[8 * h : 8 * h + 8] for h in range(2)]
            span = pl.ds(pl.multiple_of(i * ck, ck), ck)
            moe_out[:, span] = jnp.concatenate(both, axis=1).astype(bf16)

        return carry

    lax.fori_loop(0, NC + BACK_CORE + 2 * BACK_LAG, return_step, 0)

    def drain(k, carry):
        for d in range(1, line):
            send_line(k, d).wait_send()
            back_line(k, d).wait_send()
        send_pair(k).wait_send()
        send_core(k).wait_send()
        back_pair(k).wait_send()
        back_core(k).wait_send()
        return carry

    lax.fori_loop(0, NC, drain, 0)
    for d in range(1, line):
        share_line(d).wait_send()
    share_pair().wait_send()
    share_core().wait_send()


def place_outputs(moe, context, moe_out, context_out, sems):
    copies = [
        pltpu.make_async_copy(moe, moe_out, sems.at[0]),
        pltpu.make_async_copy(context, context_out, sems.at[1]),
    ]
    for copy in copies:
        copy.start()
    for copy in copies:
        copy.wait()


def fused(
    nodes,
    locals_,
    hidden_rows,
    w_router,
    chosen,
    w_gate,
    w_up,
    w_down,
    q_latent,
    q_rope,
    cache_latent,
    cache_rope,
    lengths,
):
    batch_rows, positions, latent = cache_latent.shape
    rope_width = cache_rope.shape[1]
    heads = q_latent.shape[1] // latent
    row_count, model_width = hidden_rows.shape
    ff = w_gate.shape[1]
    line = locals_ // PAIR
    total = nodes * locals_ * row_count
    ck = model_width // NC
    half = ck // 2
    vmem = pl.BlockSpec(memory_space=pltpu.VMEM)
    hbm = pl.BlockSpec(memory_space=pl.ANY)
    smem = pl.BlockSpec(memory_space=pltpu.SMEM)
    dma = pltpu.SemaphoreType.DMA
    moe_out, context = pl.pallas_call(
        functools.partial(kernel, nodes, locals_),
        out_shape=(
            jax.ShapeDtypeStruct((row_count, model_width), bf16),
            jax.ShapeDtypeStruct((batch_rows, heads * latent), bf16),
        ),
        in_specs=[vmem, vmem, vmem, hbm, hbm, hbm, vmem, vmem, hbm, hbm, smem],
        out_specs=(vmem, vmem),
        scratch_shapes=[
            pltpu.VMEM((batch_rows, heads, latent), bf16),
            pltpu.VMEM((batch_rows, heads, rope_width), bf16),
            pltpu.VMEM(cache_latent.shape, bf16),
            pltpu.VMEM(cache_rope.shape, bf16),
            pltpu.VMEM((batch_rows, heads, latent), f32),
            pltpu.VMEM((NC, nodes, PAIR, line, 16, half), bf16),
            pltpu.VMEM((nodes, PAIR, line, 8, 128), f32),
            pltpu.VMEM((NC, ck, ff), bf16),
            pltpu.VMEM((NC, ck, ff), bf16),
            pltpu.VMEM((NC, ff, ck), bf16),
            pltpu.VMEM((total, ff), f32),
            pltpu.VMEM((total, ff), f32),
            pltpu.VMEM((total, ff), bf16),
            pltpu.VMEM((NC, PAIR, line, 16, half), f32),
            pltpu.VMEM((NC, PAIR, line, 16, half), bf16),
            pltpu.VMEM((NC, PAIR, line, 16, half), bf16),
            pltpu.VMEM((NC, PAIR, line, 16, half), f32),
            pltpu.VMEM((NC, line, 16, half), bf16),
            pltpu.VMEM((NC, line, 16, half), bf16),
            pltpu.VMEM((NC, line, 16, half), f32),
            pltpu.VMEM((NC, line, 16, half), bf16),
            pltpu.VMEM((NC, line - 1, 16, half), bf16),
            dma((2,)),
            dma((NC,)),
            dma((NC,)),
            dma((NC,)),
            dma((NC, line - 1)),
            dma((NC, line - 1)),
            dma((NC,)),
            dma((NC,)),
            dma((NC,)),
            dma((NC,)),
            dma((line - 1,)),
            dma((line - 1,)),
            dma((2,)),
            dma((2,)),
            dma((NC, line - 1)),
            dma((NC, line - 1)),
            dma((NC,)),
            dma((NC,)),
            dma((NC,)),
            dma((NC,)),
        ],
        compiler_params=pltpu.CompilerParams(
            collective_id=0, has_side_effects=True, vmem_limit_bytes=62 * 1024 * 1024
        ),
    )(
        hidden_rows,
        w_router.T,
        chosen.T,
        w_gate,
        w_up,
        w_down,
        q_latent,
        q_rope,
        cache_latent,
        cache_rope,
        lengths,
    )
    return pl.pallas_call(
        place_outputs,
        out_shape=(
            jax.ShapeDtypeStruct(moe_out.shape, bf16),
            jax.ShapeDtypeStruct(context.shape, bf16),
        ),
        in_specs=[hbm, hbm],
        out_specs=(vmem, vmem),
        scratch_shapes=[dma((2,))],
    )(moe_out, context)


def solution(mesh):
    nodes, locals_ = mesh.shape["node"], mesh.shape["local"]
    spread = ("rep", "node", "local")
    return jax.shard_map(
        functools.partial(fused, nodes, locals_),
        mesh=mesh,
        in_specs=(
            P(spread, None),
            P(),
            P(spread, None),
            P(None, ("node", "local")),
            P(None, ("node", "local")),
            P(("node", "local"), None),
            P(spread, None),
            P(spread, None),
            P(spread, None, None),
            P(spread, None, None),
            P(spread),
        ),
        out_specs=(P(spread, None), P(spread, None)),
        check_vma=False,
    )
```
